32 devices in a mesh: groups: 1, dp: 16 (over z, y, x), tensor: 2 (over core).
Axes of the slice: x: 2, y: 2, z: 4, core: 2. Of those that a mesh axis runs over, the one named last changes fastest.
Arguments:
- inputs: bfloat16 [64, 4096], P(('groups', 'dp', 'tensor')), may hold values from -6 to 6
- out_grad: bfloat16 [64, 4096], P(('groups', 'dp', 'tensor')), may hold values from -0.8984375 to 0.8984375
- block_ids: int32 [64], P('groups'), may hold values from 0 to 15, never falling along the last dimension, each value on 1 to 8 neighbouring positions
- up_weight: bfloat16 [4096, 32768], P(None, ('dp', 'tensor')), may hold values from -0.09375 to 0.09375
- down_weight: bfloat16 [32768, 4096], P(('dp', 'tensor')), may hold values from -0.03125 to 0.03125
Outputs:
- input_grad: bfloat16 [64, 4096], P(('groups', 'dp', 'tensor'))
- neuron_scores: float32 [16, 32768], P('groups', ('dp', 'tensor'))
- up_grad: bfloat16 [4096, 32768], P('groups', ('dp', 'tensor'))
- down_grad: bfloat16 [32768, 4096], P(('groups', 'dp', 'tensor'))
The draws below stay inside these ranges and needn't reach their ends.
Inputs may be any that keep to these rules, and one draw needn't show every extreme that they name: `block_ids`: ids never fall along the tokens; each of the 16 samples holds 1 to 8 tokens, and one holds exactly 8.
All inputs are finite; a program needn't handle non-finite values.
Results may differ from the reference program's by a relative error of at most 0.0051.
Values may be sent and summed in bfloat16 or wider, within the bound.
A program may use at most 384 MiB of HBM per device.

```python
import math
import jax
import jax.numpy as jnp
import numpy as np
from jax import lax

D = 4096
FF = 32768
NBLK = 16
TOKENS = 64
BLK_MOST = 8


def level_of(rng, extent, pieces, smallest, top_value):
    def one(axis_at, blocks):
        steps = jax.random.uniform(jax.random.fold_in(jax.random.fold_in(rng, 6), axis_at), (blocks,), jnp.float32, smallest / len(pieces), top_value / len(pieces))
        return jnp.repeat(jnp.exp(steps), extent[axis_at] // blocks).reshape((-1,) + (1,) * (len(extent) - axis_at - 1))

    gain = one(*pieces[0])
    for cut in pieces[1:]:
        gain = gain * one(*cut)
    return gain


def profile(amount, total, most, lean):
    loads = [(1 << 20) // math.isqrt(rank ** lean) + 1 for rank in range(2, amount + 1)]
    rest, counts = total - most - (amount - 1), [1] * (amount - 1)
    while rest > 0:
        movable = [i for i in range(amount - 1) if counts[i] < most]
        pool, left = sum([loads[i] for i in movable]), rest
        for i in movable:
            addition = min(most - counts[i], max(1, left * loads[i] // pool), rest)
            counts[i] = counts[i] + addition
            rest = rest - addition
    return np.array([most] + counts)


def uneven(own_key, count, total, limit, slope):
    if count == 2:
        one = jax.random.randint(own_key, (), max(1, total - limit), min(limit, total - 1) + 1)
        return jnp.stack([one, total - one])
    sizes = jnp.asarray(profile(count, total, limit, slope), jnp.int32)
    twos = (count - 1) // 2
    source_of, sink = sizes[1:1 + 2 * twos:2], sizes[2:2 + 2 * twos:2]
    room = jnp.minimum(source_of - 1, limit - sink)
    passed = jax.random.randint(jax.random.fold_in(own_key, 1), (twos,), 0, 1 << 20) % (room + 1)
    sizes = sizes.at[1:1 + 2 * twos:2].set(source_of - passed).at[2:2 + 2 * twos:2].set(sink + passed)
    return sizes[jax.random.permutation(jax.random.fold_in(own_key, 2), count)]


def bell_draw(rng, shape, spread, bound, shards=(), held_as=jnp.bfloat16):
    result = jax.random.normal(rng, shape, jnp.float32) * spread
    if len(shards) > 0:
        result = level_of(rng, shape, shards, -0.22, 0.18) * result
    return jnp.clip(result, min=-bound, max=bound).astype(held_as)


def setup_inputs(seed: int = 0, part: int = 0) -> dict:
    seeds = jax.random.split(jax.random.key(seed), 6)
    part_keys = jax.random.split(jax.random.fold_in(seeds[5], part), 6)
    inputs = bell_draw(part_keys[0], (TOKENS, D), 1.0, 6.0, ((0, 32),))
    out_grad = bell_draw(part_keys[1], (TOKENS, D), 0.15, 0.8984375, ((0, 32),))
    block_ids = jnp.searchsorted(jnp.cumsum(uneven(part_keys[2], NBLK, TOKENS, BLK_MOST, 2)), jnp.arange(TOKENS), side="right").astype(jnp.int32)
    up_weight = bell_draw(seeds[3], (D, FF), D ** -0.5, 0.09375, ((1, 32),))
    down_weight = bell_draw(seeds[4], (FF, D), FF ** -0.5, 0.03125, ((0, 32),))
    return {"inputs": inputs, "out_grad": out_grad, "block_ids": block_ids, "up_weight": up_weight, "down_weight": down_weight}


def reference(inputs, out_grad, block_ids, up_weight, down_weight):
    pre = jnp.dot(inputs, up_weight, preferred_element_type=jnp.float32)
    positive = jnp.maximum(pre, 0.0)
    act32 = positive * positive
    activation = act32.astype(jnp.bfloat16)
    act_grad = lax.dot_general(out_grad, down_weight, (((1,), (1,)), ((), ())), preferred_element_type=jnp.float32)
    pre_grad = (2.0 * positive * act_grad).astype(jnp.bfloat16)
    input_grad = lax.dot_general(pre_grad, up_weight, (((1,), (1,)), ((), ())), preferred_element_type=jnp.float32).astype(jnp.bfloat16)
    up_grad = lax.dot_general(inputs, pre_grad, (((0,), (0,)), ((), ())), preferred_element_type=jnp.float32).astype(jnp.bfloat16)
    down_grad = lax.dot_general(activation, out_grad, (((0,), (0,)), ((), ())), preferred_element_type=jnp.float32).astype(jnp.bfloat16)
    block_onehot = (block_ids[:, None] == jnp.arange(NBLK, dtype=jnp.int32)[None, :]).astype(jnp.float32)
    sample_sums = lax.dot_general(block_onehot, act32 * act_grad, (((0,), (0,)), ((), ())), precision=lax.Precision.HIGHEST, preferred_element_type=jnp.float32)
    neuron_scores = jnp.abs(sample_sums)
    return input_grad, neuron_scores, up_grad, down_grad
```

```python
import jax
import jax.numpy as jnp
from jax import lax
from jax.sharding import PartitionSpec as P

NBLK = 16
AXES = ("dp", "tensor")


def contract_rows(left, right):
    return lax.dot_general(
        left, right, (((0,), (0,)), ((), ())), preferred_element_type=jnp.float32
    )


def on_device(inputs, out_grad, block_ids, up_weight, down_weight):
    x_rows = lax.all_gather(inputs, AXES, axis=0, tiled=True)
    g_rows = lax.all_gather(out_grad, AXES, axis=0, tiled=True)
    block_onehot = (block_ids[:, None] == jnp.arange(NBLK, dtype=jnp.int32)[None, :]).astype(
        jnp.float32
    )
    pre = jnp.dot(x_rows, up_weight, preferred_element_type=jnp.float32)
    positive = jnp.maximum(pre, 0.0)
    act32 = positive * positive
    act_grad = lax.dot_general(
        g_rows, down_weight, (((1,), (1,)), ((), ())), preferred_element_type=jnp.float32
    )
    pre_grad = (2.0 * positive * act_grad).astype(jnp.bfloat16)
    sums = lax.dot_general(
        block_onehot,
        act32 * act_grad,
        (((0,), (0,)), ((), ())),
        precision=lax.Precision.HIGHEST,
        preferred_element_type=jnp.float32,
    )
    input_grad = lax.psum_scatter(
        lax.dot_general(
            pre_grad, up_weight, (((1,), (1,)), ((), ())), preferred_element_type=jnp.float32
        ),
        AXES,
        scatter_dimension=0,
        tiled=True,
    ).astype(jnp.bfloat16)
    return (
        input_grad,
        jnp.abs(sums),
        contract_rows(x_rows, pre_grad).astype(jnp.bfloat16),
        contract_rows(act32.astype(jnp.bfloat16), g_rows).astype(jnp.bfloat16),
    )


def solution(mesh):
    return jax.shard_map(
        on_device,
        mesh=mesh,
        in_specs=(
            P(("groups", "dp", "tensor"), None),
            P(("groups", "dp", "tensor"), None),
            P("groups"),
            P(None, ("dp", "tensor")),
            P(("dp", "tensor"), None),
        ),
        out_specs=(
            P(("groups", "dp", "tensor"), None),
            P("groups", ("dp", "tensor")),
            P("groups", ("dp", "tensor")),
            P(("groups", "dp", "tensor"), None),
        ),
        check_vma=False,
    )
```

```python
import functools

import jax
import jax.numpy as jnp
from jax import lax
from jax.experimental import pallas as pl
from jax.experimental.pallas import tpu as pltpu
from jax.sharding import PartitionSpec as P

NBLK = 16
TILE = 16
MESH = pl.DeviceIdType.MESH
F32, BF16 = jnp.float32, jnp.bfloat16


def orders(count_dp):
    bits = count_dp.bit_length() - 1
    first = list(range(bits - 1, -1, -1))
    second = list(first)
    if bits >= 4:
        second[2], second[3] = second[3], second[2]
    return first, second


def position(dp, order):
    return sum(((dp // 2**b) % 2) * 2**k for k, b in enumerate(order))


def swapped(p):
    return (p & ~12) | ((p & 4) << 1) | ((p & 8) >> 1)


def permutation(group, rows, pieces, second, flip):
    size = group * TILE
    m = lax.broadcasted_iota(jnp.int32, (size, size), 1 if flip else 0)
    k = lax.broadcasted_iota(jnp.int32, (size, size), 0 if flip else 1)
    row = m & (rows - 1)
    place = (m >> (rows.bit_length() - 1)) & (group - 1)
    piece = m >> ((rows * group).bit_length() - 1)
    if second and group >= 16:
        place = swapped(place)
    return jnp.where(k == place * TILE + piece * rows + row, 1.0, 0.0).astype(BF16)


def sample_rows(ids, tokens, rows, count_dp, order):
    shape = (tokens, tokens)
    nat = lax.broadcasted_iota(jnp.int32, shape, 0)
    can = lax.broadcasted_iota(jnp.int32, shape, 1)
    shift = rows.bit_length() - 1
    place = (can >> shift) & (count_dp - 1)
    core = can >> (shift + count_dp.bit_length() - 1)
    dp = sum((((place >> k) & 1) << b for k, b in enumerate(order)), jnp.zeros_like(place))
    want = (dp * 2 + core) * rows + (can & (rows - 1))
    move = jnp.where(nat == want, 1.0, 0.0).astype(BF16)
    natural = jnp.where(
        lax.broadcasted_iota(jnp.int32, (NBLK, tokens), 0) == ids, 1.0, 0.0
    ).astype(BF16)
    return jnp.dot(natural, move, preferred_element_type=F32)


def exchange_kernel(
    count_dp, x_ref, g_ref, ids_ref, up_hbm, down_hbm,
    ig_ref, sc_ref, xa_ref, ga_ref, act_ref, pg_ref,
    upv, dnv, bufx, bufg, perm, zs, snd0, rcv0, snd, rcv, acc,
    wsem, gs, gr, cs, cr, r0s, r0r, rs, rr,
):
    rows, feats = x_ref.shape
    width = dnv.shape[0]
    tokens = xa_ref.shape[0]
    pieces = TILE // rows
    lanes = feats // pieces
    half = lanes // 2
    group = min(16, count_dp)
    groups = count_dp // group
    span = group * rows
    order = orders(count_dp)
    bits = len(order[0])
    dp = lax.axis_index("dp")
    core = lax.axis_index("tensor")
    other = 1 - core
    pos = [position(dp, o) for o in order]

    loads = []
    for i in range(4):
        a, b = feats // 4, width // 4
        loads.append(pltpu.make_async_copy(up_hbm.at[pl.ds(i * a, a)], upv.at[pl.ds(i * a, a)], wsem.at[i]))
        loads.append(pltpu.make_async_copy(down_hbm.at[pl.ds(i * b, b)], dnv.at[pl.ds(i * b, b)], wsem.at[4 + i]))
    for load in loads:
        load.start()

    def to_dp(h, bit):
        b = order[h][bit]
        side = (dp // 2**b) % 2
        return {"dp": dp + (1 - 2 * side) * 2**b}

    def remote(src, dst, s, r, device):
        copy = pltpu.make_async_remote_copy(
            src_ref=src, dst_ref=dst, send_sem=s, recv_sem=r, device_id=device, device_id_type=MESH
        )
        copy.start()
        return copy

    barrier = pltpu.get_barrier_semaphore()
    for k in range(bits):
        pl.semaphore_signal(barrier, inc=1, device_id=to_dp(0, k), device_id_type=MESH)
    pl.semaphore_signal(barrier, inc=1, device_id={"tensor": other}, device_id_type=MESH)

    bufs = (bufx, bufg)
    for h, ref in enumerate((x_ref, g_ref)):
        wide = ref[...].astype(F32)
        block = jnp.concatenate([wide[:, c * lanes:(c + 1) * lanes] for c in range(pieces)], axis=0)
        bufs[h][core, pos[h]] = block.astype(BF16)
    pl.semaphore_wait(barrier, bits + 1)

    steps = [[], []]
    shared = [[], []]

    def share(h, j, start, size):
        part = bufs[h].at[core, pl.ds(start, size)]
        shared[h].append(remote(part, part, cs.at[h, j], cr.at[h, j], {"tensor": other}))

    for k in range(bits + 1):
        for h in range(2):
            if k > 0:
                steps[h][k - 1].wait_recv()
            if k < bits:
                size = 2**k
                part = bufs[h].at[core, pl.ds((pos[h] // size) * size, size)]
                steps[h].append(remote(part, part, gs.at[h, k], gr.at[h, k], to_dp(h, k)))
            if k == 0:
                share(h, 0, pos[h], 1)
            else:
                size = 2 ** (k - 1)
                mine = pos[h] // size
                share(h, k, (mine + 1 - 2 * (mine % 2)) * size, size)
            if k == 0:
                perm[h] = permutation(group, rows, pieces, h == 1, False)
                perm[2 + h] = permutation(group, rows, pieces, h == 1, True)
    samples = sample_rows(ids_ref[...], tokens, rows, count_dp, order[0])
    for h in range(2):
        for copy in shared[h]:
            copy.wait_recv()
    for h, whole in enumerate((xa_ref, ga_ref)):
        for cc in range(2):
            for gi in range(groups):
                block = bufs[h][cc, gi * group:(gi + 1) * group].reshape(group * TILE, lanes)
                y = jnp.dot(perm[h], block, preferred_element_type=F32).astype(BF16)
                r0 = (cc * groups + gi) * span
                for c in range(pieces):
                    whole[r0:r0 + span, c * lanes:(c + 1) * lanes] = y[c * span:(c + 1) * span]
    for load in loads:
        load.wait()

    nb = min(256, width)
    for n in range(width // nb):
        cols = slice(n * nb, (n + 1) * nb)
        pre = jnp.dot(xa_ref[...], upv[:, cols], preferred_element_type=F32)
        act_grad = lax.dot_general(
            ga_ref[...], dnv[cols, :], (((1,), (1,)), ((), ())), preferred_element_type=F32
        )
        positive = jnp.maximum(pre, 0.0)
        act32 = positive * positive
        act_ref[:, cols] = act32.astype(BF16)
        pg_ref[:, cols] = (2.0 * positive * act_grad).astype(BF16)
        sc_ref[:, cols] = jnp.abs(
            jnp.dot(samples, act32 * act_grad, precision=lax.Precision.HIGHEST, preferred_element_type=F32)
        )

    for c in range(pieces):
        z = lax.dot_general(
            pg_ref[...], upv[c * lanes:(c + 1) * lanes, :], (((1,), (1,)), ((), ())),
            preferred_element_type=F32,
        ).astype(BF16)
        for cc in range(2):
            for gi in range(groups):
                r0 = (cc * groups + gi) * span
                zs[cc, gi, c * span:(c + 1) * span, :] = z[r0:r0 + span]

    def by_place(h, side, gi):
        v = jnp.dot(perm[2 + h], zs[side, gi, :, h * half:(h + 1) * half], preferred_element_type=F32)
        return v.reshape(group, TILE, half)

    pair = []
    for h in range(2):
        for gi in range(groups):
            snd0[h, gi * group:(gi + 1) * group] = by_place(h, other, gi).astype(BF16)
        pair.append(remote(snd0.at[h], rcv0.at[h], r0s.at[h], r0r.at[h], {"tensor": other}))
    for h in range(2):
        for gi in range(groups):
            acc[h, gi * group:(gi + 1) * group] = by_place(h, core, gi)
    sums = [[], []]
    for k in range(bits - 1, -1, -1):
        size = 2**k
        for h in range(2):
            side = (pos[h] // size) % 2
            base = (pos[h] // (2 * size)) * (2 * size)
            if k == bits - 1:
                pair[h].wait_recv()
                acc[h] = acc[h] + rcv0[h].astype(F32)
            else:
                sums[h][-1].wait_recv()
                now = pl.ds(base, 2 * size)
                acc[h, now] = acc[h, now] + rcv[h, 2 * size:4 * size].astype(F32)
            snd[h, size:2 * size] = acc[h, pl.ds(base + (1 - side) * size, size)].astype(BF16)
            sums[h].append(
                remote(
                    snd.at[h, pl.ds(size, size)], rcv.at[h, pl.ds(size, size)],
                    rs.at[h, k], rr.at[h, k], to_dp(h, k),
                )
            )
    last = []
    for h in range(2):
        sums[h][-1].wait_recv()
        last.append(acc[h, pos[h]] + rcv[h, 1].astype(F32))
    ig_ref[...] = jnp.concatenate(
        [last[h][c * rows:(c + 1) * rows] for c in range(pieces) for h in range(2)], axis=1
    ).astype(BF16)
    for h in range(2):
        for copy in steps[h] + shared[h] + [pair[h]] + sums[h]:
            copy.wait_send()


def weight_grads_kernel(x_ref, pg_ref, act_ref, g_ref, up_ref, down_ref):
    contract = (((0,), (0,)), ((), ()))
    up_ref[...] = lax.dot_general(x_ref[...], pg_ref[...], contract, preferred_element_type=F32).astype(BF16)
    down_ref[...] = lax.dot_general(act_ref[...], g_ref[...], contract, preferred_element_type=F32).astype(BF16)


def on_device(inputs, out_grad, block_ids, up_weight, down_weight):
    rows, feats = inputs.shape
    width = up_weight.shape[1]
    count_dp = lax.axis_size("dp")
    tokens = rows * count_dp * 2
    lanes = feats * rows // TILE
    half = lanes // 2
    group = min(16, count_dp)
    groups = count_dp // group
    bits = count_dp.bit_length() - 1
    vmem = pl.BlockSpec(memory_space=pltpu.VMEM)
    hbm = pl.BlockSpec(memory_space=pl.ANY)
    sem = pltpu.SemaphoreType.DMA
    input_grad, scores, x_all, g_all, act, pre_grad = pl.pallas_call(
        functools.partial(exchange_kernel, count_dp),
        out_shape=(
            jax.ShapeDtypeStruct((rows, feats), BF16),
            jax.ShapeDtypeStruct((NBLK, width), F32),
            jax.ShapeDtypeStruct((tokens, feats), BF16),
            jax.ShapeDtypeStruct((tokens, feats), BF16),
            jax.ShapeDtypeStruct((tokens, width), BF16),
            jax.ShapeDtypeStruct((tokens, width), BF16),
        ),
        in_specs=[vmem, vmem, vmem, hbm, hbm],
        out_specs=(vmem,) * 6,
        scratch_shapes=[
            pltpu.VMEM((feats, width), BF16),
            pltpu.VMEM((width, feats), BF16),
            pltpu.VMEM((2, count_dp, TILE, lanes), BF16),
            pltpu.VMEM((2, count_dp, TILE, lanes), BF16),
            pltpu.VMEM((4, group * TILE, group * TILE), BF16),
            pltpu.VMEM((2, groups, group * TILE, lanes), BF16),
            pltpu.VMEM((2, count_dp, TILE, half), BF16),
            pltpu.VMEM((2, count_dp, TILE, half), BF16),
            pltpu.VMEM((2, count_dp, TILE, half), BF16),
            pltpu.VMEM((2, count_dp, TILE, half), BF16),
            pltpu.VMEM((2, count_dp, TILE, half), F32),
            sem((8,)),
            sem((2, bits)), sem((2, bits)),
            sem((2, bits + 1)), sem((2, bits + 1)),
            sem((2,)), sem((2,)),
            sem((2, bits)), sem((2, bits)),
        ],
        compiler_params=pltpu.CompilerParams(
            collective_id=0, has_side_effects=True, vmem_limit_bytes=48 * 2**20
        ),
        cost_estimate=pl.CostEstimate(
            flops=6 * tokens * feats * width, bytes_accessed=4 * feats * width, transcendentals=0
        ),
        name="exchange",
    )(inputs, out_grad, block_ids.reshape(1, tokens), up_weight, down_weight)
    parts = 8
    up_grad, down_grad = pl.pallas_call(
        weight_grads_kernel,
        grid=(parts,),
        out_shape=(
            jax.ShapeDtypeStruct((feats, width), BF16),
            jax.ShapeDtypeStruct((width, feats), BF16),
        ),
        in_specs=[
            pl.BlockSpec((tokens, feats // parts), lambda i: (0, i)),
            pl.BlockSpec((tokens, width), lambda i: (0, 0)),
            pl.BlockSpec((tokens, width), lambda i: (0, 0)),
            pl.BlockSpec((tokens, feats // parts), lambda i: (0, i)),
        ],
        out_specs=(
            pl.BlockSpec((feats // parts, width), lambda i: (i, 0)),
            pl.BlockSpec((width, feats // parts), lambda i: (0, i)),
        ),
        compiler_params=pltpu.CompilerParams(vmem_limit_bytes=32 * 2**20),
        cost_estimate=pl.CostEstimate(
            flops=4 * tokens * feats * width, bytes_accessed=4 * feats * width, transcendentals=0
        ),
        name="weight_grads",
    )(x_all, pre_grad, act, g_all)
    return input_grad, scores, up_grad, down_grad


def solution(mesh):
    return jax.shard_map(
        on_device,
        mesh=mesh,
        in_specs=(
            P(("groups", "dp", "tensor"), None),
            P(("groups", "dp", "tensor"), None),
            P("groups"),
            P(None, ("dp", "tensor")),
            P(("dp", "tensor"), None),
        ),
        out_specs=(
            P(("groups", "dp", "tensor"), None),
            P("groups", ("dp", "tensor")),
            P("groups", ("dp", "tensor")),
            P(("groups", "dp", "tensor"), None),
        ),
        check_vma=False,
    )
```

```python
import functools

import jax
import jax.numpy as jnp
from jax import lax
from jax.experimental import pallas as pl
from jax.experimental.pallas import tpu as pltpu
from jax.sharding import PartitionSpec as P

NBLK = 16
TILE = 16
MESH = pl.DeviceIdType.MESH
F32, BF16 = jnp.float32, jnp.bfloat16


def permutation(group, rows, flip):
    size = group * TILE
    m = lax.broadcasted_iota(jnp.int32, (size, size), 1 if flip else 0)
    k = lax.broadcasted_iota(jnp.int32, (size, size), 0 if flip else 1)
    row = m & (rows - 1)
    place = (m >> (rows.bit_length() - 1)) & (group - 1)
    piece = m >> ((rows * group).bit_length() - 1)
    return jnp.where(k == place * TILE + piece * rows + row, 1.0, 0.0).astype(BF16)


def sample_rows(ids, tokens, rows, count_dp):
    nat = lax.broadcasted_iota(jnp.int32, (tokens, tokens), 0)
    can = lax.broadcasted_iota(jnp.int32, (tokens, tokens), 1)
    shift = rows.bit_length() - 1
    dp = (can >> shift) & (count_dp - 1)
    core = can >> (shift + count_dp.bit_length() - 1)
    want = (dp * 2 + core) * rows + (can & (rows - 1))
    move = jnp.where(nat == want, 1.0, 0.0).astype(BF16)
    natural = jnp.where(
        lax.broadcasted_iota(jnp.int32, (NBLK, tokens), 0) == ids, 1.0, 0.0
    ).astype(BF16)
    return jnp.dot(natural, move, preferred_element_type=F32)


def exchange_kernel(
    count_dp, near, xg_ref, up_hbm, down_hbm,
    ig_ref, prod_ref, xa_ref, ga_ref, act_ref, pg_ref,
    upv, dnv, buf, perm, zs, snd0, rcv0, acc, snd1, rcv1, snd2, rcv2,
    wsem, hs, hr, ls, lr, cs, cr, p0s, p0r, p1s, p1r, p2s, p2r,
):
    rows, feats = ig_ref.shape
    width = dnv.shape[0]
    pieces = TILE // rows
    lanes = feats // pieces
    group = min(16, count_dp)
    groups = count_dp // group
    span = group * rows
    far = count_dp // near
    dp = lax.axis_index("dp")
    core = lax.axis_index("tensor")
    other = 1 - core
    hi, lo = dp // near, dp % near
    steps = sorted(range(1, far), key=lambda j: (min(j, far - j), j))

    loads = []
    for i in range(4):
        a, b = feats // 4, width // 4
        loads.append(pltpu.make_async_copy(up_hbm.at[pl.ds(i * a, a)], upv.at[pl.ds(i * a, a)], wsem.at[i]))
        loads.append(pltpu.make_async_copy(down_hbm.at[pl.ds(i * b, b)], dnv.at[pl.ds(i * b, b)], wsem.at[4 + i]))
    for load in loads:
        load.start()

    def far_peer(j):
        return {"dp": (hi + j) % far * near + lo}

    def near_peer(j):
        return {"dp": hi * near + (lo + j) % near}

    sent = []

    def remote(src, dst, s, r, device):
        copy = pltpu.make_async_remote_copy(
            src_ref=src, dst_ref=dst, send_sem=s, recv_sem=r, device_id=device, device_id_type=MESH
        )
        copy.start()
        sent.append(copy)
        return copy

    barrier = pltpu.get_barrier_semaphore()
    peers = [far_peer(j) for j in range(1, far)] + [near_peer(j) for j in range(1, near)]
    for peer in peers + [{"tensor": other}]:
        pl.semaphore_signal(barrier, inc=1, device_id=peer, device_id_type=MESH)
    wide = xg_ref[...].astype(F32)
    for h in range(2):
        block = jnp.concatenate(
            [wide[h * rows:(h + 1) * rows, c * lanes:(c + 1) * lanes] for c in range(pieces)], axis=0
        )
        buf[core, dp, h] = block.astype(BF16)
    pl.semaphore_wait(barrier, len(peers) + 1)

    own = buf.at[core, dp]
    over_far = {j: remote(own, own, hs.at[j - 1], hr.at[j - 1], far_peer(j)) for j in steps}
    over_near, shared = {}, []

    def pass_on(j, place):
        part = buf.at[core, place]
        for i in range(1, near):
            over_near[j, i] = remote(part, part, ls.at[j, i - 1], lr.at[j, i - 1], near_peer(i))
        share(j, 0, place)

    def share(j, i, place):
        part = buf.at[core, place]
        shared.append(remote(part, part, cs.at[j, i], cr.at[j, i], {"tensor": other}))

    pass_on(0, dp)
    perm[0] = permutation(group, rows, False)
    perm[1] = permutation(group, rows, True)
    for j in steps:
        over_far[j].wait_recv()
        pass_on(j, (hi + far - j) % far * near + lo)
    for j in [0] + steps:
        for i in range(1, near):
            over_near[j, i].wait_recv()
            share(j, i, (hi + far - j) % far * near + (lo + near - i) % near)
    for copy in shared:
        copy.wait_recv()

    for h, whole in enumerate((xa_ref, ga_ref)):
        for cc in range(2):
            for gi in range(groups):
                block = buf[cc, gi * group:(gi + 1) * group, h].reshape(group * TILE, lanes)
                y = jnp.dot(perm[0], block, preferred_element_type=F32).astype(BF16)
                r0 = (cc * groups + gi) * span
                for c in range(pieces):
                    whole[r0:r0 + span, c * lanes:(c + 1) * lanes] = y[c * span:(c + 1) * span]
    for load in loads:
        load.wait()

    nb = min(256, width)
    for n in range(width // nb):
        cols = slice(n * nb, (n + 1) * nb)
        pre = jnp.dot(xa_ref[...], upv[:, cols], preferred_element_type=F32)
        act_grad = lax.dot_general(
            ga_ref[...], dnv[cols, :], (((1,), (1,)), ((), ())), preferred_element_type=F32
        )
        positive = jnp.maximum(pre, 0.0)
        act32 = positive * positive
        act_ref[:, cols] = act32.astype(BF16)
        pg_ref[:, cols] = (2.0 * positive * act_grad).astype(BF16)
        prod_ref[:, cols] = act32 * act_grad

    for c in range(pieces):
        z = lax.dot_general(
            pg_ref[...], upv[c * lanes:(c + 1) * lanes, :], (((1,), (1,)), ((), ())),
            preferred_element_type=F32,
        ).astype(BF16)
        for cc in range(2):
            for gi in range(groups):
                r0 = (cc * groups + gi) * span
                zs[cc, gi, c * span:(c + 1) * span, :] = z[r0:r0 + span]

    def by_place(side, gi):
        v = jnp.dot(perm[1], zs[side, gi], preferred_element_type=F32)
        return v.reshape(group, TILE, lanes)

    for gi in range(groups):
        snd0[gi * group:(gi + 1) * group] = by_place(other, gi).astype(BF16)
    order = steps[::-1] + [0]
    pair = {}
    for j in order:
        block = pl.ds((hi + j) % far * near, near)
        pair[j] = remote(snd0.at[block], rcv0.at[block], p0s.at[j], p0r.at[j], {"tensor": other})
    for gi in range(groups):
        acc[gi * group:(gi + 1) * group] = by_place(core, gi)
    to_near, to_far = {}, {}
    for j in order:
        start = (hi + j) % far * near
        block = pl.ds(start, near)
        pair[j].wait_recv()
        both = acc[block] + rcv0[block].astype(F32)
        acc[block] = both
        snd1[block] = both.astype(BF16)
        for i in range(1, near):
            to_near[j, i] = remote(
                snd1.at[start + (lo + i) % near], rcv1.at[j, i - 1],
                p1s.at[j, i - 1], p1r.at[j, i - 1], near_peer(i),
            )
    total = None
    for j in order:
        total = acc[(hi + j) % far * near + lo]
        for i in range(1, near):
            to_near[j, i].wait_recv()
            total = total + rcv1[j, i - 1].astype(F32)
        if j > 0:
            snd2[j - 1] = total.astype(BF16)
            to_far[j] = remote(snd2.at[j - 1], rcv2.at[j - 1], p2s.at[j - 1], p2r.at[j - 1], far_peer(j))
    for j in order[:-1]:
        to_far[j].wait_recv()
        total = total + rcv2[j - 1].astype(F32)
    ig_ref[...] = jnp.concatenate([total[c * rows:(c + 1) * rows] for c in range(pieces)], axis=1)
    for copy in sent:
        copy.wait_send()


def weight_grads_kernel(
    count_dp, sum_ref, prod_ref, ids_ref, x_ref, pg_ref, act_ref, g_ref,
    ig_ref, sc_ref, up_ref, down_ref,
):
    @pl.when(pl.program_id(0) == 0)
    def _():
        rows, tokens = ig_ref.shape[0], ids_ref.shape[1]
        ig_ref[...] = sum_ref[...].astype(BF16)
        samples = sample_rows(ids_ref[...], tokens, rows, count_dp)
        sc_ref[...] = jnp.abs(
            jnp.dot(samples, prod_ref[...], precision=lax.Precision.HIGHEST, preferred_element_type=F32)
        )

    contract = (((0,), (0,)), ((), ()))
    up_ref[...] = lax.dot_general(x_ref[...], pg_ref[...], contract, preferred_element_type=F32).astype(BF16)
    down_ref[...] = lax.dot_general(act_ref[...], g_ref[...], contract, preferred_element_type=F32).astype(BF16)


def on_device(inputs, out_grad, block_ids, up_weight, down_weight):
    rows, feats = inputs.shape
    width = up_weight.shape[1]
    count_dp = lax.axis_size("dp")
    tokens = rows * count_dp * 2
    lanes = feats * rows // TILE
    group = min(16, count_dp)
    groups = count_dp // group
    near = min(4, count_dp)
    far = count_dp // near
    vmem = pl.BlockSpec(memory_space=pltpu.VMEM)
    hbm = pl.BlockSpec(memory_space=pl.ANY)
    sem = pltpu.SemaphoreType.DMA
    in_sums, products, x_all, g_all, act, pre_grad = pl.pallas_call(
        functools.partial(exchange_kernel, count_dp, near),
        out_shape=(
            jax.ShapeDtypeStruct((rows, feats), F32),
            jax.ShapeDtypeStruct((tokens, width), F32),
            jax.ShapeDtypeStruct((tokens, feats), BF16),
            jax.ShapeDtypeStruct((tokens, feats), BF16),
            jax.ShapeDtypeStruct((tokens, width), BF16),
            jax.ShapeDtypeStruct((tokens, width), BF16),
        ),
        in_specs=[vmem, hbm, hbm],
        out_specs=(vmem,) * 6,
        scratch_shapes=[
            pltpu.VMEM((feats, width), BF16),
            pltpu.VMEM((width, feats), BF16),
            pltpu.VMEM((2, count_dp, 2, TILE, lanes), BF16),
            pltpu.VMEM((2, group * TILE, group * TILE), BF16),
            pltpu.VMEM((2, groups, group * TILE, lanes), BF16),
            pltpu.VMEM((count_dp, TILE, lanes), BF16),
            pltpu.VMEM((count_dp, TILE, lanes), BF16),
            pltpu.VMEM((count_dp, TILE, lanes), F32),
            pltpu.VMEM((count_dp, TILE, lanes), BF16),
            pltpu.VMEM((far, near - 1, TILE, lanes), BF16),
            pltpu.VMEM((far - 1, TILE, lanes), BF16),
            pltpu.VMEM((far - 1, TILE, lanes), BF16),
            sem((8,)),
            sem((far - 1,)), sem((far - 1,)),
            sem((far, near - 1)), sem((far, near - 1)),
            sem((far, near)), sem((far, near)),
            sem((far,)), sem((far,)),
            sem((far, near - 1)), sem((far, near - 1)),
            sem((far - 1,)), sem((far - 1,)),
        ],
        compiler_params=pltpu.CompilerParams(
            collective_id=0, has_side_effects=True, vmem_limit_bytes=48 * 2**20
        ),
        cost_estimate=pl.CostEstimate(
            flops=6 * tokens * feats * width, bytes_accessed=4 * feats * width, transcendentals=0
        ),
        name="exchange",
    )(jnp.concatenate([inputs, out_grad], axis=0), up_weight, down_weight)
    parts = 8
    fixed = lambda i: (0, 0)
    return pl.pallas_call(
        functools.partial(weight_grads_kernel, count_dp),
        grid=(parts,),
        out_shape=(
            jax.ShapeDtypeStruct((rows, feats), BF16),
            jax.ShapeDtypeStruct((NBLK, width), F32),
            jax.ShapeDtypeStruct((feats, width), BF16),
            jax.ShapeDtypeStruct((width, feats), BF16),
        ),
        in_specs=[
            pl.BlockSpec((rows, feats), fixed),
            pl.BlockSpec((tokens, width), fixed),
            pl.BlockSpec((1, tokens), fixed),
            pl.BlockSpec((tokens, feats // parts), lambda i: (0, i)),
            pl.BlockSpec((tokens, width), fixed),
            pl.BlockSpec((tokens, width), fixed),
            pl.BlockSpec((tokens, feats // parts), lambda i: (0, i)),
        ],
        out_specs=(
            pl.BlockSpec((rows, feats), fixed),
            pl.BlockSpec((NBLK, width), fixed),
            pl.BlockSpec((feats // parts, width), lambda i: (i, 0)),
            pl.BlockSpec((width, feats // parts), lambda i: (0, i)),
        ),
        compiler_params=pltpu.CompilerParams(vmem_limit_bytes=32 * 2**20),
        cost_estimate=pl.CostEstimate(
            flops=4 * tokens * feats * width, bytes_accessed=4 * feats * width, transcendentals=0
        ),
        name="weight_grads",
    )(in_sums, products, block_ids.reshape(1, tokens), x_all, pre_grad, act, g_all)


def solution(mesh):
    return jax.shard_map(
        on_device,
        mesh=mesh,
        in_specs=(
            P(("groups", "dp", "tensor"), None),
            P(("groups", "dp", "tensor"), None),
            P("groups"),
            P(None, ("dp", "tensor")),
            P(("dp", "tensor"), None),
        ),
        out_specs=(
            P(("groups", "dp", "tensor"), None),
            P("groups", ("dp", "tensor")),
            P("groups", ("dp", "tensor")),
            P(("groups", "dp", "tensor"), None),
        ),
        check_vma=False,
    )
```

```python
import functools

import jax
import jax.numpy as jnp
from jax import lax
from jax.experimental import pallas as pl
from jax.experimental.pallas import tpu as pltpu
from jax.sharding import PartitionSpec as P

NBLK = 16
TILE = 16
MESH = pl.DeviceIdType.MESH
F32, BF16 = jnp.float32, jnp.bfloat16


def permutation(group, rows, flip):
    size = group * TILE
    m = lax.broadcasted_iota(jnp.int32, (size, size), 1 if flip else 0)
    k = lax.broadcasted_iota(jnp.int32, (size, size), 0 if flip else 1)
    row = m & (rows - 1)
    place = (m >> (rows.bit_length() - 1)) & (group - 1)
    piece = m >> ((rows * group).bit_length() - 1)
    return jnp.where(k == place * TILE + piece * rows + row, 1.0, 0.0).astype(BF16)


def sample_rows(ids, tokens, rows, count_dp):
    nat = lax.broadcasted_iota(jnp.int32, (tokens, tokens), 0)
    can = lax.broadcasted_iota(jnp.int32, (tokens, tokens), 1)
    shift = rows.bit_length() - 1
    dp = (can >> shift) & (count_dp - 1)
    core = can >> (shift + count_dp.bit_length() - 1)
    want = (dp * 2 + core) * rows + (can & (rows - 1))
    move = jnp.where(nat == want, 1.0, 0.0).astype(BF16)
    natural = jnp.where(
        lax.broadcasted_iota(jnp.int32, (NBLK, tokens), 0) == ids, 1.0, 0.0
    ).astype(BF16)
    return jnp.dot(natural, move, preferred_element_type=F32)


def exchange_kernel(
    count_dp, near, xg_ref, up_hbm, down_hbm,
    ig_ref, prod_ref, xa_ref, ga_ref, act_ref, pg_ref,
    upv, dnv, buf, perm, zs, snd0, rcv0, acc, snd1, rcv1, snd2, rcv2,
    wsem, hs, hr, ls, lr, cs, cr, p0s, p0r, p1s, p1r, p2s, p2r,
):
    rows, feats = ig_ref.shape
    width = dnv.shape[0]
    pieces = TILE // rows
    lanes = feats // pieces
    group = min(16, count_dp)
    groups = count_dp // group
    span = group * rows
    far = count_dp // near
    dp = lax.axis_index("dp")
    core = lax.axis_index("tensor")
    other = 1 - core
    hi, lo = dp // near, dp % near
    steps = sorted(range(1, far), key=lambda j: (min(j, far - j), j))

    loads = []
    for i in range(4):
        a, b = feats // 4, width // 4
        loads.append(pltpu.make_async_copy(up_hbm.at[pl.ds(i * a, a)], upv.at[pl.ds(i * a, a)], wsem.at[i]))
        loads.append(pltpu.make_async_copy(down_hbm.at[pl.ds(i * b, b)], dnv.at[pl.ds(i * b, b)], wsem.at[4 + i]))
    for load in loads:
        load.start()

    def far_peer(j):
        return {"dp": (hi + j) % far * near + lo}

    def near_peer(j):
        return {"dp": hi * near + (lo + j) % near}

    sent = []

    def remote(src, dst, s, r, device):
        copy = pltpu.make_async_remote_copy(
            src_ref=src, dst_ref=dst, send_sem=s, recv_sem=r, device_id=device, device_id_type=MESH
        )
        copy.start()
        sent.append(copy)
        return copy

    barrier = pltpu.get_barrier_semaphore()
    peers = [far_peer(j) for j in range(1, far)] + [near_peer(j) for j in range(1, near)]
    for peer in peers + [{"tensor": other}]:
        pl.semaphore_signal(barrier, inc=1, device_id=peer, device_id_type=MESH)
    wide = xg_ref[...].astype(F32)
    for h in range(2):
        block = jnp.concatenate(
            [wide[h * rows:(h + 1) * rows, c * lanes:(c + 1) * lanes] for c in range(pieces)], axis=0
        )
        buf[core, dp, h] = block.astype(BF16)
    pl.semaphore_wait(barrier, len(peers) + 1)

    own = buf.at[core, dp]
    over_far = {j: remote(own, own, hs.at[j - 1], hr.at[j - 1], far_peer(j)) for j in steps}
    over_near, shared = {}, []

    def pass_on(j, place):
        part = buf.at[core, place]
        for i in range(1, near):
            over_near[j, i] = remote(part, part, ls.at[j, i - 1], lr.at[j, i - 1], near_peer(i))
        share(j, 0, place)

    def share(j, i, place):
        part = buf.at[core, place]
        shared.append(remote(part, part, cs.at[j, i], cr.at[j, i], {"tensor": other}))

    pass_on(0, dp)
    perm[0] = permutation(group, rows, False)
    perm[1] = permutation(group, rows, True)
    for j in steps:
        over_far[j].wait_recv()
        pass_on(j, (hi + far - j) % far * near + lo)
    for j in [0] + steps:
        for i in range(1, near):
            over_near[j, i].wait_recv()
            share(j, i, (hi + far - j) % far * near + (lo + near - i) % near)
    for copy in shared:
        copy.wait_recv()

    for h, whole in enumerate((xa_ref, ga_ref)):
        for cc in range(2):
            for gi in range(groups):
                block = buf[cc, gi * group:(gi + 1) * group, h].reshape(group * TILE, lanes)
                y = jnp.dot(perm[0], block, preferred_element_type=F32).astype(BF16)
                r0 = (cc * groups + gi) * span
                for c in range(pieces):
                    whole[r0:r0 + span, c * lanes:(c + 1) * lanes] = y[c * span:(c + 1) * span]
    for load in loads:
        load.wait()

    nb = min(256, width)
    for n in range(width // nb):
        cols = slice(n * nb, (n + 1) * nb)
        pre = jnp.dot(xa_ref[...], upv[:, cols], preferred_element_type=F32)
        act_grad = lax.dot_general(
            ga_ref[...], dnv[cols, :], (((1,), (1,)), ((), ())), preferred_element_type=F32
        )
        positive = jnp.maximum(pre, 0.0)
        act32 = positive * positive
        act_ref[:, cols] = act32.astype(BF16)
        pg_ref[:, cols] = (2.0 * positive * act_grad).astype(BF16)
        prod_ref[:, cols] = act32 * act_grad

    for c in range(pieces):
        z = lax.dot_general(
            pg_ref[...], upv[c * lanes:(c + 1) * lanes, :], (((1,), (1,)), ((), ())),
            preferred_element_type=F32,
        ).astype(BF16)
        for cc in range(2):
            for gi in range(groups):
                r0 = (cc * groups + gi) * span
                zs[cc, gi, c * span:(c + 1) * span, :] = z[r0:r0 + span]

    def by_place(side, gi):
        v = jnp.dot(perm[1], zs[side, gi], preferred_element_type=F32)
        return v.reshape(group, TILE, lanes)

    for gi in range(groups):
        snd0[gi * group:(gi + 1) * group] = by_place(other, gi).astype(BF16)
    order = steps[::-1] + [0]
    pair = {}
    for j in order:
        block = pl.ds((hi + j) % far * near, near)
        pair[j] = remote(snd0.at[block], rcv0.at[block], p0s.at[j], p0r.at[j], {"tensor": other})
    for gi in range(groups):
        acc[gi * group:(gi + 1) * group] = by_place(core, gi)
    to_near, to_far = {}, {}
    for j in order:
        start = (hi + j) % far * near
        block = pl.ds(start, near)
        pair[j].wait_recv()
        both = acc[block] + rcv0[block].astype(F32)
        acc[block] = both
        snd1[block] = both.astype(BF16)
        for i in range(1, near):
            to_near[j, i] = remote(
                snd1.at[start + (lo + i) % near], rcv1.at[j, i - 1],
                p1s.at[j, i - 1], p1r.at[j, i - 1], near_peer(i),
            )
    total = None
    for j in order:
        total = acc[(hi + j) % far * near + lo]
        for i in range(1, near):
            to_near[j, i].wait_recv()
            total = total + rcv1[j, i - 1].astype(F32)
        if j > 0:
            snd2[j - 1] = total.astype(BF16)
            to_far[j] = remote(snd2.at[j - 1], rcv2.at[j - 1], p2s.at[j - 1], p2r.at[j - 1], far_peer(j))
    for j in order[:-1]:
        to_far[j].wait_recv()
        total = total + rcv2[j - 1].astype(F32)
    ig_ref[...] = jnp.concatenate([total[c * rows:(c + 1) * rows] for c in range(pieces)], axis=1)
    for copy in sent:
        copy.wait_send()


def weight_grads_kernel(
    count_dp, sum_ref, prod_ref, ids_ref, x_ref, pg_ref, act_ref, g_ref,
    ig_ref, sc_ref, up_ref, down_ref,
):
    @pl.when(pl.program_id(0) == 0)
    def _():
        rows, tokens = ig_ref.shape[0], ids_ref.shape[1]
        ig_ref[...] = sum_ref[...].astype(BF16)
        samples = sample_rows(ids_ref[...], tokens, rows, count_dp)
        sc_ref[...] = jnp.abs(
            jnp.dot(samples, prod_ref[...], precision=lax.Precision.HIGHEST, preferred_element_type=F32)
        )

    contract = (((0,), (0,)), ((), ()))
    up_ref[...] = lax.dot_general(x_ref[...], pg_ref[...], contract, preferred_element_type=F32).astype(BF16)
    down_ref[...] = lax.dot_general(act_ref[...], g_ref[...], contract, preferred_element_type=F32).astype(BF16)


def on_device(inputs, out_grad, block_ids, up_weight, down_weight):
    rows, feats = inputs.shape
    width = up_weight.shape[1]
    count_dp = lax.axis_size("dp")
    tokens = rows * count_dp * 2
    lanes = feats * rows // TILE
    group = min(16, count_dp)
    groups = count_dp // group
    near = min(4, count_dp)
    far = count_dp // near
    vmem = pl.BlockSpec(memory_space=pltpu.VMEM)
    hbm = pl.BlockSpec(memory_space=pl.ANY)
    sem = pltpu.SemaphoreType.DMA
    in_sums, products, x_all, g_all, act, pre_grad = pl.pallas_call(
        functools.partial(exchange_kernel, count_dp, near),
        out_shape=(
            jax.ShapeDtypeStruct((rows, feats), F32),
            jax.ShapeDtypeStruct((tokens, width), F32),
            jax.ShapeDtypeStruct((tokens, feats), BF16),
            jax.ShapeDtypeStruct((tokens, feats), BF16),
            jax.ShapeDtypeStruct((tokens, width), BF16),
            jax.ShapeDtypeStruct((tokens, width), BF16),
        ),
        in_specs=[vmem, hbm, hbm],
        out_specs=(vmem,) * 6,
        scratch_shapes=[
            pltpu.VMEM((feats, width), BF16),
            pltpu.VMEM((width, feats), BF16),
            pltpu.VMEM((2, count_dp, 2, TILE, lanes), BF16),
            pltpu.VMEM((2, group * TILE, group * TILE), BF16),
            pltpu.VMEM((2, groups, group * TILE, lanes), BF16),
            pltpu.VMEM((count_dp, TILE, lanes), BF16),
            pltpu.VMEM((count_dp, TILE, lanes), BF16),
            pltpu.VMEM((count_dp, TILE, lanes), F32),
            pltpu.VMEM((count_dp, TILE, lanes), BF16),
            pltpu.VMEM((far, near - 1, TILE, lanes), BF16),
            pltpu.VMEM((far - 1, TILE, lanes), BF16),
            pltpu.VMEM((far - 1, TILE, lanes), BF16),
            sem((8,)),
            sem((far - 1,)), sem((far - 1,)),
            sem((far, near - 1)), sem((far, near - 1)),
            sem((far, near)), sem((far, near)),
            sem((far,)), sem((far,)),
            sem((far, near - 1)), sem((far, near - 1)),
            sem((far - 1,)), sem((far - 1,)),
        ],
        compiler_params=pltpu.CompilerParams(
            collective_id=0, has_side_effects=True, vmem_limit_bytes=48 * 2**20
        ),
        cost_estimate=pl.CostEstimate(
            flops=6 * tokens * feats * width, bytes_accessed=4 * feats * width, transcendentals=0
        ),
        name="exchange",
    )(jnp.concatenate([inputs, out_grad], axis=0), up_weight, down_weight)
    parts = 4
    act_parts = min(parts, width // 128)
    fixed = lambda i: (0, 0)
    return pl.pallas_call(
        functools.partial(weight_grads_kernel, count_dp),
        grid=(parts,),
        out_shape=(
            jax.ShapeDtypeStruct((rows, feats), BF16),
            jax.ShapeDtypeStruct((NBLK, width), F32),
            jax.ShapeDtypeStruct((feats, width), BF16),
            jax.ShapeDtypeStruct((width, feats), BF16),
        ),
        in_specs=[
            pl.BlockSpec((rows, feats), fixed),
            pl.BlockSpec((tokens, width), fixed),
            pl.BlockSpec((1, tokens), fixed),
            pl.BlockSpec((tokens, feats // parts), lambda i: (0, i)),
            pl.BlockSpec((tokens, width), fixed),
            pl.BlockSpec((tokens, width // act_parts), lambda i: (0, i * act_parts // parts)),
            pl.BlockSpec((tokens, feats * act_parts // parts), lambda i: (0, i % (parts // act_parts))),
        ],
        out_specs=(
            pl.BlockSpec((rows, feats), fixed),
            pl.BlockSpec((NBLK, width), fixed),
            pl.BlockSpec((feats // parts, width), lambda i: (i, 0)),
            pl.BlockSpec((width // act_parts, feats * act_parts // parts), lambda i: (i * act_parts // parts, i % (parts // act_parts))),
        ),
        compiler_params=pltpu.CompilerParams(vmem_limit_bytes=32 * 2**20),
        cost_estimate=pl.CostEstimate(
            flops=4 * tokens * feats * width, bytes_accessed=4 * feats * width, transcendentals=0
        ),
        name="weight_grads",
    )(in_sums, products, block_ids.reshape(1, tokens), x_all, pre_grad, act, g_all)


def solution(mesh):
    return jax.shard_map(
        on_device,
        mesh=mesh,
        in_specs=(
            P(("groups", "dp", "tensor"), None),
            P(("groups", "dp", "tensor"), None),
            P("groups"),
            P(None, ("dp", "tensor")),
            P(("dp", "tensor"), None),
        ),
        out_specs=(
            P(("groups", "dp", "tensor"), None),
            P("groups", ("dp", "tensor")),
            P("groups", ("dp", "tensor")),
            P(("groups", "dp", "tensor"), None),
        ),
        check_vma=False,
    )
```
